32 devices in a mesh: dp: 16 (over z, y, core), mp: 2 (over x).
Axes of the slice: x: 2, y: 2, z: 4, core: 2. Of those that a mesh axis runs over, the one named last changes fastest.
Arguments:
- image: bfloat16 [1152, 8192], P(None, ('dp', 'mp')), may hold values from -0.29882812 to 0.29882812
- text: bfloat16 [1152, 8192], P(None, ('dp', 'mp')), may hold values from -0.29882812 to 0.29882812
- scale: float32 [1], replicated, may hold values from 5 to 15
- bias: float32 [1], replicated, may hold values from -5 to -3
Outputs:
- grad_image: float32 [1152, 8192], P(None, ('dp', 'mp'))
- row_loss: float32 [8192], P(('dp', 'mp'))
- grad_text: float32 [1152, 8192], P(None, ('dp', 'mp'))
The draws below stay inside these ranges and needn't reach their ends.
All inputs are finite; a program needn't handle non-finite values.
Results may differ from the reference program's by a relative error of at most 0.0022.
Values may be sent and summed in bfloat16 or wider, within the bound.
No kernel may reach another device: no remote copies, remote signals or barrier semaphores. Data moves between devices by JAX's collectives and lax.ppermute only.
A program may use at most 64 MiB of HBM per device.

```python
import jax
import jax.numpy as jnp
from jax import lax

D = 1152
ROWS_DEV = 256
WINDOW = 8
BATCH = 8192
N_DP = 16
N_MP = 2


def level_of(own_key, extent, split, least, largest):
    def one(position, blocks):
        steps = jax.random.uniform(jax.random.fold_in(jax.random.fold_in(own_key, 6), position), (blocks,), jnp.float32, least / len(split), largest / len(split))
        return jnp.repeat(jnp.exp(steps), extent[position] // blocks).reshape((-1,) + (1,) * (len(extent) - position - 1))

    gain = one(*split[0])
    for cut in split[1:]:
        gain = gain * one(*cut)
    return gain


def gaussian(stream_key, dims, deviation, reach, shards=(), dtype=jnp.bfloat16):
    level = level_of(stream_key, dims, shards, -0.22, 0.18) if shards else 1.0
    entries = jax.random.normal(stream_key, dims, jnp.float32) * deviation * level
    return jnp.minimum(jnp.maximum(entries, -reach), reach).astype(dtype)


def setup_inputs(seed: int = 0) -> dict:
    arg_keys = jax.random.split(jax.random.key(seed), 5)
    return {
        "image": gaussian(arg_keys[0], (D, BATCH), 0.05, 0.29882812, ((1, 32),)),
        "text": gaussian(arg_keys[1], (D, BATCH), 0.05, 0.29882812, ((1, 32),)),
        "scale": jnp.clip(jax.random.uniform(arg_keys[2], (1,), jnp.float32, 5.0, 15.0), 5.0, 15.0),
        "bias": jnp.clip(jax.random.uniform(arg_keys[3], (1,), jnp.float32, -5.0, -3.0), -5.0, -3.0),
    }


def reference(image, text, scale, bias):
    rows = ROWS_DEV
    groups = N_DP * N_MP
    images = image.T.reshape(groups, rows, D)
    texts = text.T.reshape(groups, rows, D)
    temper = scale[0]
    offset = bias[0]
    ident = (jnp.arange(rows)[:, None] == jnp.arange(rows)[None, :]).astype(jnp.float32)
    grad_img = jnp.zeros((groups, rows, D), jnp.float32)
    grad_txt = jnp.zeros((groups, rows, D), jnp.float32)
    losses = jnp.zeros((groups, rows), jnp.float32)
    for step in range(WINDOW):
        shifted = jnp.roll(texts, step, axis=0)
        positive = ident if step == 0 else jnp.zeros_like(ident)

        def block(pair):
            left, right = pair
            inner = lax.dot_general(left, right, (((1,), (1,)), ((), ())), preferred_element_type=jnp.float32)
            logits = temper * inner + offset
            grad_logit = (jax.nn.sigmoid(logits) - positive).astype(jnp.bfloat16)
            row_terms = jnp.sum(jax.nn.softplus(logits) - positive * logits, axis=1)
            grad_left = temper * jnp.dot(grad_logit, right, preferred_element_type=jnp.float32)
            grad_right = temper * jnp.dot(grad_logit.T, left, preferred_element_type=jnp.float32)
            return grad_left, row_terms, grad_right

        grad_left, row_terms, grad_right = lax.map(block, (images, shifted))
        grad_img = grad_img + grad_left
        losses = losses + row_terms
        grad_txt = grad_txt + jnp.roll(grad_right, -step, axis=0)
    return grad_img.reshape(groups * rows, D).T, (losses / float(rows)).reshape(groups * rows), grad_txt.reshape(groups * rows, D).T
```

```python
import functools

import jax
import jax.numpy as jnp
from jax import lax
from jax.experimental import pallas as pl
from jax.experimental.pallas import tpu as pltpu
from jax.sharding import PartitionSpec as P

AXES = ("dp", "mp")
WINDOW = 8
PAIR, CORE, SIDE = 1, 2, 4
MASKS = (0, CORE, PAIR, CORE | PAIR)
EXTRA = 16
VMEM_BYTES = 40 * 1024 * 1024

NN = (((1,), (0,)), ((), ()))
NT = (((1,), (1,)), ((), ()))


def dot(a, b, dims):
    return lax.dot_general(a, b, dims, preferred_element_type=jnp.float32)


def moved(block, target):
    n = lax.axis_size(AXES)
    route = [(i, target(i, n)) for i in range(n) if target(i, n) is not None]
    return lax.ppermute(block, AXES, route)


def forward(i, n):
    return (i + WINDOW) % n


def back(i, n):
    return (i - WINDOW) % n


def swap(mask):
    return lambda i, n: i ^ mask


def to_high(i, n):
    return None if i & SIDE else i | SIDE


def to_low(i, n):
    return i ^ SIDE if i & SIDE else None


def terms(inner, temper, offset):
    z = temper * inner + offset
    e = jnp.exp(-jnp.abs(z))
    r = 1.0 / (1.0 + e)
    return z, jnp.where(z >= 0, r, e * r), jnp.maximum(z, 0.0) + jnp.log1p(e)


def partner_kernel(start, tb, i0, i1, i2, i3, whole, part, grad_x, grad, loss, kept):
    temper, offset = tb[0], tb[1]
    cols = part.shape[1]
    text = whole[:, start : start + cols] + part[...]
    kept[...] = text
    turned = text.T
    images = (i0, i1, i2, i3)
    for r, image in enumerate(images):
        _, s, soft = terms(dot(turned, image[...], NN), temper, offset)
        grad[r] = s.astype(jnp.bfloat16)
        loss[r : r + 1] = jnp.sum(soft, axis=0, keepdims=True)
    tile = 384
    for d in range(0, text.shape[0], tile):
        total = dot(i0[d : d + tile], grad[0], NT)
        for r in (1, 2, 3):
            total = total + dot(images[r][d : d + tile], grad[r], NT)
        grad_x[d : d + tile] = (temper * total).astype(jnp.bfloat16)


def own_kernel(tb, later, i0, i1, i2, i3, text, m1, m2, grad_t, grad_m1, grad_m2, grad, loss, kept, turned, masked):
    temper, offset = tb[0], tb[1]
    rows = text.shape[1]
    half = rows // 2
    kept[0] = text[...]
    kept[1, :, :half] = m1[...]
    kept[1, :, half:] = m2[...]
    turned[0] = text[...].T
    turned[1, :half] = m1[...].T
    turned[1, half:] = m2[...].T
    images = (i0, i1, i2, i3)
    for r, image in enumerate(images):
        same = later[r]
        z, s, soft = terms(dot(turned[1 - same], image[...], NN), temper, offset)
        if r == 0:
            diag = lax.broadcasted_iota(jnp.int32, z.shape, 0) == lax.broadcasted_iota(jnp.int32, z.shape, 1)
            s = jnp.where(diag, s - 1.0, s)
            soft = jnp.where(diag, soft - z, soft)
        g = s.astype(jnp.bfloat16)
        grad[r] = g
        loss[r : r + 1] = jnp.sum(soft, axis=0, keepdims=True)
        masked[0, r] = jnp.where(same == 1, g, jnp.zeros_like(g))
        masked[1, r] = jnp.where(same == 1, jnp.zeros_like(g), g)
    tile = 384
    for d in range(0, text.shape[0], tile):
        total = dot(i0[d : d + tile], masked[0, 0], NT)
        for r in (1, 2, 3):
            total = total + dot(images[r][d : d + tile], masked[0, r], NT)
        grad_t[d : d + tile] = temper * total
        total = dot(i1[d : d + tile], masked[1, 1], NT)
        for r in (2, 3):
            total = total + dot(images[r][d : d + tile], masked[1, r], NT)
        total = temper * total
        grad_m1[d : d + tile] = total[:, :half]
        grad_m2[d : d + tile] = total[:, half:]


def row_total(r, tb, later, kept, k1, k2, g, g1, g2, d, tile):
    same = later[r]
    total = dot(kept[1 - same, d : d + tile], g[r], NN)
    total = total + dot(k1[d : d + tile], g1[r], NN)
    total = total + dot(k2[d : d + tile], g2[r], NN)
    return tb[0] * total


def split_loss(r, l0, l1, l2, shape):
    value = l0[r : r + 1] + l1[r : r + 1] + l2[r : r + 1]
    high = value.astype(jnp.bfloat16).astype(jnp.float32)
    place = lax.broadcasted_iota(jnp.int32, shape, 0)
    value, high = jnp.broadcast_to(value, shape), jnp.broadcast_to(high, shape)
    return jnp.where(place == 0, high, jnp.where(place == 1, value - high, 0.0))


def away_kernel(tb, later, kept, k1, k2, g, g1, g2, l0, l1, l2, out):
    width = k1.shape[0]
    tile = 384
    for slot, r in enumerate((1, 3)):
        for d in range(0, width, tile):
            out[slot, d : d + tile] = row_total(r, tb, later, kept, k1, k2, g, g1, g2, d, tile).astype(jnp.bfloat16)
        out[slot, width:] = split_loss(r, l0, l1, l2, out[slot, width:].shape).astype(jnp.bfloat16)


def home_kernel(tb, later, kept, k1, k2, g, g1, g2, l0, l1, l2, out, loss):
    width = k1.shape[0]
    tile = 384
    for slot, r in enumerate((0, 2)):
        for d in range(0, width, tile):
            out[slot, d : d + tile] = row_total(r, tb, later, kept, k1, k2, g, g1, g2, d, tile)
        loss[slot : slot + 1] = l0[r : r + 1] + l1[r : r + 1] + l2[r : r + 1]


def joined_kernel(home, loss, came, out):
    width = home.shape[1]
    out[:width] = (home[1] + came[1, :width].astype(jnp.float32)).astype(jnp.bfloat16)
    shape = (EXTRA, home.shape[2])
    tail = came[1, width:].astype(jnp.float32)
    value = loss[1:2] + tail[0:1] + tail[1:2]
    high = value.astype(jnp.bfloat16).astype(jnp.float32)
    place = lax.broadcasted_iota(jnp.int32, shape, 0)
    value, high = jnp.broadcast_to(value, shape), jnp.broadcast_to(high, shape)
    out[width:] = jnp.where(place == 0, high, jnp.where(place == 1, value - high, 0.0)).astype(jnp.bfloat16)


def call(kernel, out_shape, args, scratch=(), flops=0):
    spaces = [pltpu.SMEM if a.ndim == 1 else pltpu.VMEM for a in args]
    return pl.pallas_call(
        kernel,
        out_shape=out_shape,
        in_specs=[pl.BlockSpec(memory_space=s) for s in spaces],
        out_specs=jax.tree.map(lambda _: pl.BlockSpec(memory_space=pltpu.VMEM), out_shape),
        scratch_shapes=list(scratch),
        compiler_params=pltpu.CompilerParams(vmem_limit_bytes=VMEM_BYTES),
        cost_estimate=pl.CostEstimate(flops=flops, bytes_accessed=sum(a.size * a.dtype.itemsize for a in args), transcendentals=0),
    )(*args)


def shards(image, text, scale, bias):
    width, rows = image.shape
    half = rows // 2
    f32, bf16 = jnp.float32, jnp.bfloat16
    sds = jax.ShapeDtypeStruct
    place = lax.axis_index(AXES) % WINDOW
    tb = jnp.concatenate([scale, bias])
    later = jnp.stack([((place ^ m) >= place).astype(jnp.int32) for m in MASKS])
    unit = 2 * rows * rows * width

    m1 = moved(text[:, :half], forward)
    m2 = moved(text[:, half:], forward)
    low = moved(text, to_high)
    image_c = moved(image, swap(CORE))
    image_p = moved(image, swap(PAIR))
    x1 = moved(m1, to_low)
    x2 = moved(m2, to_low)
    image_pc = moved(image_p, swap(CORE))
    images = (image, image_c, image_p, image_pc)

    def partner(start, part):
        return call(
            functools.partial(partner_kernel, start),
            (sds((width, half), bf16), sds((4, half, rows), bf16), sds((8, rows), f32), sds((width, half), bf16)),
            (tb, *images, low, part),
            flops=4 * unit,
        )

    grad_x1, g1, l1, k1 = partner(0, x1)
    grad_t, grad_m1, grad_m2, g0, l0, kept = call(
        own_kernel,
        (
            sds((width, rows), f32),
            sds((width, half), f32),
            sds((width, half), f32),
            sds((4, rows, rows), bf16),
            sds((8, rows), f32),
            sds((2, width, rows), bf16),
        ),
        (tb, later, *images, text, m1, m2),
        scratch=(pltpu.VMEM((2, rows, width), bf16), pltpu.VMEM((2, 4, rows, rows), bf16)),
        flops=11 * unit,
    )
    grad_x2, g2, l2, k2 = partner(half, x2)

    up1 = moved(grad_x1, to_high)
    up2 = moved(grad_x2, to_high)
    down1 = moved(grad_x1, to_low)
    down2 = moved(grad_x2, to_low)
    past1 = moved((grad_m1 + up1).astype(bf16), back)
    past2 = moved((grad_m2 + up2).astype(bf16), back)

    rest = (tb, later, kept, k1, k2, g0, g1, g2, l0, l1, l2)
    away = call(away_kernel, sds((2, width + EXTRA, rows), bf16), rest, flops=4 * unit)
    came = moved(away, swap(CORE))
    home, home_loss = call(home_kernel, (sds((2, width, rows), f32), sds((8, rows), f32)), rest, flops=4 * unit)
    joined = call(joined_kernel, sds((width + EXTRA, rows), bf16), (home, home_loss, came))
    other = moved(joined, swap(PAIR))

    grad_image = home[0] + came[0, :width].astype(f32) + other[:width].astype(f32)
    losses = home_loss[0] + jnp.sum(came[0, width : width + 2].astype(f32), axis=0) + jnp.sum(other[width : width + 2].astype(f32), axis=0)
    downs = jnp.concatenate([down1.astype(f32) + past1.astype(f32), down2.astype(f32) + past2.astype(f32)], axis=1)
    return grad_image, losses / float(rows), grad_t + downs


def solution(mesh):
    spread = P(None, AXES)
    return jax.shard_map(
        shards,
        mesh=mesh,
        in_specs=(spread, spread, P(), P()),
        out_specs=(spread, P(AXES), spread),
        check_vma=False,
    )
```

```python
import functools

import jax
import jax.numpy as jnp
from jax import lax
from jax.experimental import pallas as pl
from jax.experimental.pallas import tpu as pltpu
from jax.sharding import PartitionSpec as P

AXES = ("dp", "mp")
WINDOW = 8
PAIR, CORE, SIDE = 1, 2, 4
MASKS = (0, CORE, PAIR, CORE | PAIR)
EXTRA = 16
VMEM_BYTES = 20 * 1024 * 1024

NN = (((1,), (0,)), ((), ()))
NT = (((1,), (1,)), ((), ()))


def dot(a, b, dims):
    return lax.dot_general(a, b, dims, preferred_element_type=jnp.float32)


def moved(block, target):
    n = lax.axis_size(AXES)
    return lax.ppermute(block, AXES, [(i, target(i, n)) for i in range(n)])


def forward(i, n):
    return (i + WINDOW) % n


def back(i, n):
    return (i - WINDOW) % n


def swap(mask):
    return lambda i, n: i ^ mask


def terms(inner, temper, offset):
    z = temper * inner + offset
    e = jnp.exp(-jnp.abs(z))
    r = 1.0 / (1.0 + e)
    return z, jnp.where(z >= 0, r, e * r), jnp.maximum(z, 0.0) + jnp.log1p(e)


def partner_kernel(tb, i0, i1, i2, i3, text, grad_x, grad, loss):
    temper, offset = tb[0], tb[1]
    turned = text[...].T
    images = (i0, i1, i2, i3)
    for r, image in enumerate(images):
        _, s, soft = terms(dot(turned, image[...], NN), temper, offset)
        grad[r] = s.astype(jnp.bfloat16)
        loss[r : r + 1] = jnp.sum(soft, axis=0, keepdims=True)
    tile = 384
    for d in range(0, text.shape[0], tile):
        total = dot(i0[d : d + tile], grad[0], NT)
        for r in (1, 2, 3):
            total = total + dot(images[r][d : d + tile], grad[r], NT)
        grad_x[d : d + tile] = (temper * total).astype(jnp.bfloat16)


def own_kernel(tb, later, i0, i1, i2, i3, text, m1, m2, grad_t, grad_m1, grad_m2, grad, loss, kept, turned, masked):
    temper, offset = tb[0], tb[1]
    rows = text.shape[1]
    half = rows // 2
    kept[0] = text[...]
    kept[1, :, :half] = m1[...]
    kept[1, :, half:] = m2[...]
    turned[0] = text[...].T
    turned[1, :half] = m1[...].T
    turned[1, half:] = m2[...].T
    images = (i0, i1, i2, i3)
    for r, image in enumerate(images):
        same = later[r]
        z, s, soft = terms(dot(turned[1 - same], image[...], NN), temper, offset)
        if r == 0:
            diag = lax.broadcasted_iota(jnp.int32, z.shape, 0) == lax.broadcasted_iota(jnp.int32, z.shape, 1)
            s = jnp.where(diag, s - 1.0, s)
            soft = jnp.where(diag, soft - z, soft)
        g = s.astype(jnp.bfloat16)
        grad[r] = g
        loss[r : r + 1] = jnp.sum(soft, axis=0, keepdims=True)
        masked[0, r] = jnp.where(same == 1, g, jnp.zeros_like(g))
        masked[1, r] = jnp.where(same == 1, jnp.zeros_like(g), g)
    tile = 384
    for d in range(0, text.shape[0], tile):
        total = dot(i0[d : d + tile], masked[0, 0], NT)
        for r in (1, 2, 3):
            total = total + dot(images[r][d : d + tile], masked[0, r], NT)
        grad_t[d : d + tile] = temper * total
        total = dot(i1[d : d + tile], masked[1, 1], NT)
        for r in (2, 3):
            total = total + dot(images[r][d : d + tile], masked[1, r], NT)
        total = temper * total
        grad_m1[d : d + tile] = total[:, :half]
        grad_m2[d : d + tile] = total[:, half:]


def halves_kernel(text, first, second):
    half = first.shape[1]
    first[...] = text[:, :half]
    second[...] = text[:, half:]


def row_total(r, tb, later, kept, k1, k2, g, g1, g2, d, tile):
    same = later[r]
    total = dot(kept[1 - same, d : d + tile], g[r], NN)
    total = total + dot(k1[d : d + tile], g1[r], NN)
    total = total + dot(k2[d : d + tile], g2[r], NN)
    return tb[0] * total


def away_kernel(tb, later, kept, k1, k2, g, g1, g2, l0, l1, l2, out):
    width = k1.shape[0]
    tile = 384
    for slot, r in enumerate((1, 3)):
        for d in range(0, width, tile):
            out[slot, d : d + tile] = row_total(r, tb, later, kept, k1, k2, g, g1, g2, d, tile).astype(jnp.bfloat16)
        out[slot, width:] = packed_loss(l0[r : r + 1] + l1[r : r + 1] + l2[r : r + 1], (EXTRA, out.shape[2]))


def home_kernel(tb, later, kept, k1, k2, g, g1, g2, l0, l1, l2, out, loss):
    width = k1.shape[0]
    tile = 384
    for slot, r in enumerate((0, 2)):
        for d in range(0, width, tile):
            out[slot, d : d + tile] = row_total(r, tb, later, kept, k1, k2, g, g1, g2, d, tile)
        loss[slot : slot + 1] = l0[r : r + 1] + l1[r : r + 1] + l2[r : r + 1]


def packed_loss(value, shape):
    high = value.astype(jnp.bfloat16).astype(jnp.float32)
    place = lax.broadcasted_iota(jnp.int32, shape, 0)
    value, high = jnp.broadcast_to(value, shape), jnp.broadcast_to(high, shape)
    return jnp.where(place == 0, high, jnp.where(place == 1, value - high, 0.0)).astype(jnp.bfloat16)


def unpacked_loss(rows):
    rows = rows.astype(jnp.float32)
    return rows[0:1] + rows[1:2]


def joined_kernel(home, loss, came, out):
    width = home.shape[1]
    out[:width] = (home[1] + came[1, :width].astype(jnp.float32)).astype(jnp.bfloat16)
    out[width:] = packed_loss(loss[1:2] + unpacked_loss(came[1, width:]), (EXTRA, home.shape[2]))


def last_kernel(parts, later, home, loss, came, other, grad_t, r1, r2, p1, p2, grad_image, losses, grad_text, image_buf, loss_buf, text_buf, sems):
    width, rows = grad_text.shape
    half = rows // 2
    low = later[len(MASKS)] == 0
    step = width // parts
    copies = []

    def send(source, target, sem):
        copy = pltpu.make_async_copy(source, target, sems.at[sem])
        copy.start()
        copies.append(copy)

    f32 = jnp.float32
    for k in range(parts):
        d = pl.ds(k * step, step)
        image_buf[d] = home[0, d] + came[0, d].astype(f32) + other[d].astype(f32)
        send(image_buf.at[d], grad_image.at[d], k)
        text_buf[d, :half] = grad_t[d, :half] + jnp.where(low, r1[d].astype(f32), 0.0) + p1[d].astype(f32)
        text_buf[d, half:] = grad_t[d, half:] + jnp.where(low, r2[d].astype(f32), 0.0) + p2[d].astype(f32)
        send(text_buf.at[d], grad_text.at[d], parts + k)
    loss_buf[...] = (loss[0:1] + unpacked_loss(came[0, width:]) + unpacked_loss(other[width:])) / float(rows)
    send(loss_buf, losses, 2 * parts)
    for copy in copies:
        copy.wait()


def call(kernel, out_shape, args, scratch=(), flops=0, out_space=pltpu.VMEM):
    spaces = [pltpu.SMEM if a.ndim == 1 else pltpu.VMEM for a in args]
    return pl.pallas_call(
        kernel,
        out_shape=out_shape,
        in_specs=[pl.BlockSpec(memory_space=s) for s in spaces],
        out_specs=jax.tree.map(lambda _: pl.BlockSpec(memory_space=out_space), out_shape),
        scratch_shapes=list(scratch),
        cost_estimate=pl.CostEstimate(flops=flops, bytes_accessed=0, transcendentals=0),
        compiler_params=pltpu.CompilerParams(vmem_limit_bytes=VMEM_BYTES),
    )(*args)


def shards(image, text, scale, bias):
    width, rows = image.shape
    half = rows // 2
    f32, bf16 = jnp.float32, jnp.bfloat16
    sds = jax.ShapeDtypeStruct
    place = lax.axis_index(AXES) % WINDOW
    tb = jnp.concatenate([scale, bias])
    later = jnp.stack([((place ^ m) >= place).astype(jnp.int32) for m in MASKS] + [(place >= SIDE).astype(jnp.int32)])
    unit = 2 * rows * rows * width

    high = place >= SIDE
    t1, t2 = call(halves_kernel, (sds((width, half), bf16),) * 2, (text,))
    sent, t1, t2 = lax.optimization_barrier((image, t1, t2))
    m1 = moved(t1, forward)
    m2 = moved(t2, forward)
    image_p = moved(sent, swap(PAIR))
    image_c = moved(sent, swap(CORE))
    x1 = moved(jnp.where(high, m1, t1), swap(SIDE))
    x2 = moved(jnp.where(high, m2, t2), swap(SIDE))
    image_pc = moved(image_p, swap(CORE))
    images = (image, image_c, image_p, image_pc)

    def partner(part):
        return call(
            partner_kernel,
            (sds((width, half), bf16), sds((4, half, rows), bf16), sds((8, rows), f32)),
            (tb, *images, part),
            flops=4 * unit,
        )

    grad_x1, g1, l1 = partner(x1)
    late2, _ = lax.optimization_barrier((m2, l1))
    grad_t, grad_m1, grad_m2, g0, l0, kept = call(
        own_kernel,
        (
            sds((width, rows), f32),
            sds((width, half), f32),
            sds((width, half), f32),
            sds((4, rows, rows), bf16),
            sds((8, rows), f32),
            sds((2, width, rows), bf16),
        ),
        (tb, later, *images, text, m1, late2),
        scratch=(pltpu.VMEM((2, rows, width), bf16), pltpu.VMEM((2, 4, rows, rows), bf16)),
        flops=11 * unit,
    )
    x2, _ = lax.optimization_barrier((x2, l0))
    grad_x2, g2, l2 = partner(x2)

    r1 = moved(grad_x1, swap(SIDE))
    r2 = moved(grad_x2, swap(SIDE))
    rest = (tb, later, kept, x1, x2, g0, g1, g2, l0, l1, l2)
    away = call(away_kernel, sds((2, width + EXTRA, rows), bf16), rest, flops=4 * unit)
    came = moved(away, swap(CORE))
    _, l2 = lax.optimization_barrier((r1, l2))
    rest = (tb, later, kept, x1, x2, g0, g1, g2, l0, l1, l2)
    home, home_loss = call(home_kernel, (sds((2, width, rows), f32), sds((8, rows), f32)), rest, flops=120 * unit)
    joined = call(joined_kernel, sds((width + EXTRA, rows), bf16), (home, home_loss, came))
    other = moved(joined, swap(PAIR))
    past1 = moved((grad_m1 + jnp.where(high, r1.astype(f32), 0.0)).astype(bf16), back)
    past2 = moved((grad_m2 + jnp.where(high, r2.astype(f32), 0.0)).astype(bf16), back)
    parts = 4
    grad_image, losses, grad_text = call(
        functools.partial(last_kernel, parts),
        (sds((width, rows), f32), sds((1, rows), f32), sds((width, rows), f32)),
        (later, home, home_loss, came, other, grad_t, r1, r2, past1, past2),
        scratch=(
            pltpu.VMEM((width, rows), f32),
            pltpu.VMEM((1, rows), f32),
            pltpu.VMEM((width, rows), f32),
            pltpu.SemaphoreType.DMA((2 * parts + 1,)),
        ),
        out_space=pl.ANY,
    )
    return grad_image, losses.reshape(rows), grad_text


def solution(mesh):
    spread = P(None, AXES)
    return jax.shard_map(
        shards,
        mesh=mesh,
        in_specs=(spread, spread, P(), P()),
        out_specs=(spread, P(AXES), spread),
        check_vma=False,
    )
```

```python
import functools

import jax
import jax.numpy as jnp
from jax import lax
from jax.experimental import pallas as pl
from jax.experimental.pallas import tpu as pltpu
from jax.sharding import PartitionSpec as P

AXES = ("dp", "mp")
WINDOW = 8
PAIR, CORE, SIDE = 1, 2, 4
MASKS = (0, CORE, PAIR, CORE | PAIR)
EXTRA = 16
TILE = 384
VMEM_BYTES = 20 * 1024 * 1024

NN = (((1,), (0,)), ((), ()))
NT = (((1,), (1,)), ((), ()))


def dot(a, b, dims):
    return lax.dot_general(a, b, dims, preferred_element_type=jnp.float32)


def moved(block, target):
    n = lax.axis_size(AXES)
    return lax.ppermute(block, AXES, [(i, target(i, n)) for i in range(n)])


def forward(i, n):
    return (i + WINDOW) % n


def back(i, n):
    return (i - WINDOW) % n


def swap(mask):
    return lambda i, n: i ^ mask


GROUP = 8


def terms(inner, tb):
    z = tb[0] * inner + tb[1]
    e = jnp.exp(-jnp.abs(z))
    u = 1.0 + e
    r = pl.reciprocal(u, approx=True)
    r = r * (2.0 - u * r)
    product = e[:GROUP]
    positive = jnp.maximum(z[:GROUP], 0.0)
    for d in range(GROUP, z.shape[0], GROUP):
        product = product * u[d : d + GROUP] + e[d : d + GROUP]
        positive = positive + jnp.maximum(z[d : d + GROUP], 0.0)
    soft = jnp.sum(jnp.log1p(product) + positive, axis=0, keepdims=True)
    return z, jnp.where(z >= 0, r, e * r), soft


def scores(tb, images, turned, grad, loss):
    for r, image in enumerate(images):
        _, s, soft = terms(dot(turned, image[...], NN), tb)
        grad[r] = s.astype(jnp.bfloat16)
        loss[r : r + 1] = soft


def text_side(tb, images, grad, out):
    for d in range(0, out.shape[0], TILE):
        total = dot(images[0][d : d + TILE], grad[0], NT)
        for r in (1, 2, 3):
            total = total + dot(images[r][d : d + TILE], grad[r], NT)
        out[d : d + TILE] = (tb[0] * total).astype(jnp.bfloat16)


def partner_kernel(tb, i0, i1, i2, i3, text, grad_x, grad, loss):
    scores(tb, (i0, i1, i2, i3), text[...].T, grad, loss)
    text_side(tb, (i0, i1, i2, i3), grad, grad_x)


def text_kernel(tb, i0, i1, i2, i3, grad, grad_x):
    text_side(tb, (i0, i1, i2, i3), grad, grad_x)


def own_kernel(tb, later, i0, i1, i2, i3, text, m1, m2, grad_t, grad_m1, grad_m2, grad, loss, kept, turned, masked):
    temper = tb[0]
    rows = text.shape[1]
    half = rows // 2
    kept[0] = text[...]
    kept[1, :, :half] = m1[...]
    kept[1, :, half:] = m2[...]
    turned[0] = text[...].T
    turned[1, :half] = m1[...].T
    turned[1, half:] = m2[...].T
    images = (i0, i1, i2, i3)
    for r, image in enumerate(images):
        same = later[r]
        z, s, soft = terms(dot(turned[1 - same], image[...], NN), tb)
        if r == 0:
            diag = lax.broadcasted_iota(jnp.int32, z.shape, 0) == lax.broadcasted_iota(jnp.int32, z.shape, 1)
            s = jnp.where(diag, s - 1.0, s)
            soft = soft - jnp.sum(jnp.where(diag, z, 0.0), axis=0, keepdims=True)
        g = s.astype(jnp.bfloat16)
        grad[r] = g
        loss[r : r + 1] = soft
        masked[0, r] = jnp.where(same == 1, g, jnp.zeros_like(g))
        masked[1, r] = jnp.where(same == 1, jnp.zeros_like(g), g)
    for d in range(0, text.shape[0], TILE):
        total = dot(i0[d : d + TILE], masked[0, 0], NT)
        for r in (1, 2, 3):
            total = total + dot(images[r][d : d + TILE], masked[0, r], NT)
        grad_t[d : d + TILE] = temper * total
        total = dot(i1[d : d + TILE], masked[1, 1], NT)
        for r in (2, 3):
            total = total + dot(images[r][d : d + TILE], masked[1, r], NT)
        total = temper * total
        grad_m1[d : d + TILE] = total[:, :half]
        grad_m2[d : d + TILE] = total[:, half:]


def halves_kernel(text, first, second):
    half = first.shape[1]
    first[...] = text[:, :half]
    second[...] = text[:, half:]


def packed_loss(value, shape):
    high = value.astype(jnp.bfloat16).astype(jnp.float32)
    place = lax.broadcasted_iota(jnp.int32, shape, 0)
    value, high = jnp.broadcast_to(value, shape), jnp.broadcast_to(high, shape)
    return jnp.where(place == 0, high, jnp.where(place == 1, value - high, 0.0)).astype(jnp.bfloat16)


def unpacked_loss(rows):
    rows = rows.astype(jnp.float32)
    return rows[0:1] + rows[1:2]


def early_kernel(which, later, kept, k1, g, g1, part):
    for slot, r in enumerate(which):
        column = 1 - later[r]
        for d in range(0, k1.shape[0], TILE):
            part[slot, d : d + TILE] = dot(kept[column, d : d + TILE], g[r], NN) + dot(k1[d : d + TILE], g1[r], NN)


def away_kernel(tb, i0, i1, i2, i3, text, part, l0, l1, grad, loss, out):
    scores(tb, (i0, i1, i2, i3), text[...].T, grad, loss)
    width = text.shape[0]
    for slot, r in enumerate((1, 3)):
        for d in range(0, width, TILE):
            out[slot, d : d + TILE] = (tb[0] * (part[slot, d : d + TILE] + dot(text[d : d + TILE], grad[r], NN))).astype(jnp.bfloat16)
        out[slot, width:] = packed_loss(l0[r : r + 1] + l1[r : r + 1] + loss[r : r + 1], (EXTRA, out.shape[2]))


def joined_kernel(tb, text, part, grad, l0, l1, l2, came, out):
    width = text.shape[0]
    for d in range(0, width, TILE):
        total = tb[0] * (part[1, d : d + TILE] + dot(text[d : d + TILE], grad[2], NN))
        out[d : d + TILE] = (total + came[1, d : d + TILE].astype(jnp.float32)).astype(jnp.bfloat16)
    loss = l0[2:3] + l1[2:3] + l2[2:3] + unpacked_loss(came[1, width:])
    out[width:] = packed_loss(loss, (EXTRA, out.shape[1]))


def home_kernel(tb, text, part, grad, l0, l1, l2, came, out, loss):
    width = text.shape[0]
    for d in range(0, width, TILE):
        total = tb[0] * (part[0, d : d + TILE] + dot(text[d : d + TILE], grad[0], NN))
        out[d : d + TILE] = total + came[0, d : d + TILE].astype(jnp.float32)
    loss[0:1] = l0[0:1] + l1[0:1] + l2[0:1] + unpacked_loss(came[0, width:])


def older_kernel(later, grad_m, returned, out):
    high = later[len(MASKS)] == 1
    out[...] = (grad_m[...] + jnp.where(high, returned[...].astype(jnp.float32), 0.0)).astype(jnp.bfloat16)


def last_kernel(parts, later, grad_t, r1, r2, p1, p2, home, loss, other, grad_image, losses, grad_text, image_buf, loss_buf, text_buf, sems):
    width, rows = grad_text.shape
    half, step = rows // 2, width // parts
    low = later[len(MASKS)] == 0
    f32 = jnp.float32
    copies = []

    def send(source, target):
        copy = pltpu.make_async_copy(source, target, sems.at[len(copies)])
        copy.start()
        copies.append(copy)

    for k in range(parts):
        d = pl.ds(k * step, step)
        image_buf[d] = home[d] + other[d].astype(f32)
        send(image_buf.at[d], grad_image.at[d])
    loss_buf[...] = (loss[0:1] + unpacked_loss(other[width:])) / float(rows)
    send(loss_buf, losses)
    for k in range(parts):
        d = pl.ds(k * step, step)
        text_buf[d, :half] = grad_t[d, :half] + jnp.where(low, r1[d].astype(f32), 0.0) + p1[d].astype(f32)
        text_buf[d, half:] = grad_t[d, half:] + jnp.where(low, r2[d].astype(f32), 0.0) + p2[d].astype(f32)
        send(text_buf.at[d], grad_text.at[d])
    for copy in copies:
        copy.wait()


def call(kernel, out_shape, args, scratch=(), flops=0, out_space=pltpu.VMEM):
    spaces = [pltpu.SMEM if a.ndim == 1 else pltpu.VMEM for a in args]
    return pl.pallas_call(
        kernel,
        out_shape=out_shape,
        in_specs=[pl.BlockSpec(memory_space=s) for s in spaces],
        out_specs=jax.tree.map(lambda _: pl.BlockSpec(memory_space=out_space), out_shape),
        scratch_shapes=list(scratch),
        cost_estimate=pl.CostEstimate(flops=flops, bytes_accessed=0, transcendentals=0) if flops else None,
        compiler_params=pltpu.CompilerParams(vmem_limit_bytes=VMEM_BYTES),
    )(*args)


def shards(image, text, scale, bias):
    width, rows = image.shape
    half = rows // 2
    f32, bf16 = jnp.float32, jnp.bfloat16
    sds = jax.ShapeDtypeStruct
    place = lax.axis_index(AXES) % WINDOW
    tb = jnp.concatenate([scale, bias])
    later = jnp.stack([((place ^ m) >= place).astype(jnp.int32) for m in MASKS] + [(place >= SIDE).astype(jnp.int32)])
    unit = 2 * rows * rows * width

    high = place >= SIDE
    t1, t2 = call(halves_kernel, (sds((width, half), bf16),) * 2, (text,))
    sent, t1, t2 = lax.optimization_barrier((image, t1, t2))
    m1 = moved(t1, forward)
    m2 = moved(t2, forward)
    image_p = moved(sent, swap(PAIR))
    image_c = moved(sent, swap(CORE))
    x1 = moved(jnp.where(high, m1, t1), swap(SIDE))
    x2 = moved(jnp.where(high, m2, t2), swap(SIDE))
    image_pc = moved(image_p, swap(CORE))
    images = (image, image_c, image_p, image_pc)

    grad_t, grad_m1, grad_m2, g0, l0, kept = call(
        own_kernel,
        (
            sds((width, rows), f32),
            sds((width, half), f32),
            sds((width, half), f32),
            sds((4, rows, rows), bf16),
            sds((8, rows), f32),
            sds((2, width, rows), bf16),
        ),
        (tb, later, *images, text, m1, m2),
        scratch=(pltpu.VMEM((2, rows, width), bf16), pltpu.VMEM((2, 4, rows, rows), bf16)),
    )
    x1, _ = lax.optimization_barrier((x1, l0))
    scored = (sds((4, half, rows), bf16), sds((8, rows), f32))
    grad_x1, g1, l1 = call(partner_kernel, (sds((width, half), bf16), *scored), (tb, *images, x1))
    part = call(functools.partial(early_kernel, (1, 3)), sds((2, width, rows), f32), (later, kept, x1, g0, g1))
    g2, l2, away = call(away_kernel, (*scored, sds((2, width + EXTRA, rows), bf16)), (tb, *images, x2, part, l0, l1))
    came = moved(away, swap(CORE))
    grad_x2 = call(text_kernel, sds((width, half), bf16), (tb, *images, g2))
    _, held1 = lax.optimization_barrier((grad_x2, g1))
    part = call(functools.partial(early_kernel, (0, 2)), sds((2, width, rows), f32), (later, kept, x1, g0, held1))
    r1 = moved(grad_x1, swap(SIDE))
    r2 = moved(grad_x2, swap(SIDE))

    older = sds((width, half), bf16)
    older1 = call(older_kernel, older, (later, grad_m1, r1), flops=80 * unit)
    _, held = lax.optimization_barrier((older1, l2))
    joined = call(joined_kernel, sds((width + EXTRA, rows), bf16), (tb, x2, part, g2, l0, l1, held, came), flops=0 * unit)
    other = moved(joined, swap(PAIR))
    older1, grad_m2, _ = lax.optimization_barrier((older1, grad_m2, joined))
    past1 = moved(older1, back)
    past2 = moved(call(older_kernel, older, (later, grad_m2, r2), flops=20 * unit), back)
    _, late = lax.optimization_barrier((past1, l2))
    rest = (tb, x2, part, g2, l0, l1, late, came)
    home, home_loss = call(home_kernel, (sds((width, rows), f32), sds((8, rows), f32)), rest, flops=5 * unit)
    parts = 4
    grad_image, losses, grad_text = call(
        functools.partial(last_kernel, parts),
        (sds((width, rows), f32), sds((1, rows), f32), sds((width, rows), f32)),
        (later, grad_t, r1, r2, past1, past2, home, home_loss, other),
        scratch=(
            pltpu.VMEM((width, rows), f32),
            pltpu.VMEM((1, rows), f32),
            pltpu.VMEM((width, rows), f32),
            pltpu.SemaphoreType.DMA((2 * parts + 1,)),
        ),
        out_space=pl.ANY,
    )
    return grad_image, losses.reshape(rows), grad_text


def solution(mesh):
    spread = P(None, AXES)
    return jax.shard_map(
        shards,
        mesh=mesh,
        in_specs=(spread, spread, P(), P()),
        out_specs=(spread, P(AXES), spread),
        check_vma=False,
    )
```

```python
import functools

import jax
import jax.numpy as jnp
from jax import lax
from jax.experimental import pallas as pl
from jax.experimental.pallas import tpu as pltpu
from jax.sharding import PartitionSpec as P

AXES = ("dp", "mp")
WINDOW = 8
PAIR, CORE, SIDE = 1, 2, 4
MASKS = (0, CORE, PAIR, CORE | PAIR)
EXTRA = 16
TILE = 384
VMEM_BYTES = 20 * 1024 * 1024

NN = (((1,), (0,)), ((), ()))
NT = (((1,), (1,)), ((), ()))


def dot(a, b, dims):
    return lax.dot_general(a, b, dims, preferred_element_type=jnp.float32)


def moved(block, target):
    n = lax.axis_size(AXES)
    return lax.ppermute(block, AXES, [(i, target(i, n)) for i in range(n)])


def forward(i, n):
    return (i + WINDOW) % n


def back(i, n):
    return (i - WINDOW) % n


def swap(mask):
    return lambda i, n: i ^ mask


GROUP = 8


def terms(inner, tb):
    z = tb[0] * inner + tb[1]
    e = jnp.exp(-jnp.abs(z))
    u = 1.0 + e
    r = pl.reciprocal(u, approx=True)
    r = r * (2.0 - u * r)
    product = e[:GROUP]
    positive = jnp.maximum(z[:GROUP], 0.0)
    for d in range(GROUP, z.shape[0], GROUP):
        product = product * u[d : d + GROUP] + e[d : d + GROUP]
        positive = positive + jnp.maximum(z[d : d + GROUP], 0.0)
    soft = jnp.sum(jnp.log1p(product) + positive, axis=0, keepdims=True)
    return z, jnp.where(z >= 0, r, e * r), soft


def scores(tb, images, turned, grad, loss):
    for r, image in enumerate(images):
        _, s, soft = terms(dot(turned, image[...], NN), tb)
        grad[r] = s.astype(jnp.bfloat16)
        loss[r : r + 1] = soft


def text_side(tb, images, grad, out):
    for d in range(0, out.shape[0], TILE):
        total = dot(images[0][d : d + TILE], grad[0], NT)
        for r in (1, 2, 3):
            total = total + dot(images[r][d : d + TILE], grad[r], NT)
        out[d : d + TILE] = (tb[0] * total).astype(jnp.bfloat16)


def partner_kernel(tb, i0, i1, i2, i3, upper, lower, grad_x, grad, loss, text):
    cut = upper.shape[0]
    text[:cut] = upper[...]
    text[cut:] = lower[...]
    scores(tb, (i0, i1, i2, i3), text[...].T, grad, loss)
    text_side(tb, (i0, i1, i2, i3), grad, grad_x)


def text_kernel(tb, i0, i1, i2, i3, grad, grad_x):
    text_side(tb, (i0, i1, i2, i3), grad, grad_x)


def own_kernel(tb, later, i0, i1, i2, i3, text, m1a, m1b, m2, grad_m1, grad_m2, grad, loss, kept, turned, masked):
    temper = tb[0]
    rows = text.shape[1]
    half = rows // 2
    kept[0] = text[...]
    cut = m1a.shape[0]
    kept[1, :cut, :half] = m1a[...]
    kept[1, cut:, :half] = m1b[...]
    kept[1, :, half:] = m2[...]
    turned[0] = text[...].T
    turned[1, :half, :cut] = m1a[...].T
    turned[1, :half, cut:] = m1b[...].T
    turned[1, half:] = m2[...].T
    images = (i0, i1, i2, i3)
    for r, image in enumerate(images):
        same = later[r]
        z, s, soft = terms(dot(turned[1 - same], image[...], NN), tb)
        if r == 0:
            diag = lax.broadcasted_iota(jnp.int32, z.shape, 0) == lax.broadcasted_iota(jnp.int32, z.shape, 1)
            s = jnp.where(diag, s - 1.0, s)
            soft = soft - jnp.sum(jnp.where(diag, z, 0.0), axis=0, keepdims=True)
        g = s.astype(jnp.bfloat16)
        grad[r] = g
        loss[r : r + 1] = soft
        masked[r] = jnp.where(same == 1, jnp.zeros_like(g), g)
    for d in range(0, text.shape[0], TILE):
        total = dot(i1[d : d + TILE], masked[1], NT)
        for r in (2, 3):
            total = total + dot(images[r][d : d + TILE], masked[r], NT)
        total = temper * total
        grad_m1[d : d + TILE] = total[:, :half]
        grad_m2[d : d + TILE] = total[:, half:]


def own_text_kernel(tb, later, i0, i1, i2, i3, grad, grad_t, masked):
    images = (i0, i1, i2, i3)
    for r in (1, 2, 3):
        masked[r] = jnp.where(later[r] == 1, grad[r], jnp.zeros(grad.shape[1:], grad.dtype))
    for d in range(0, grad_t.shape[0], TILE):
        total = dot(i0[d : d + TILE], grad[0], NT)
        for r in (1, 2, 3):
            total = total + dot(images[r][d : d + TILE], masked[r], NT)
        grad_t[d : d + TILE] = tb[0] * total


def halves_kernel(text, upper, lower, second):
    half, cut = second.shape[1], upper.shape[0]
    upper[...] = text[:cut, :half]
    lower[...] = text[cut:, :half]
    second[...] = text[:, half:]


def packed_loss(value, shape):
    high = value.astype(jnp.bfloat16).astype(jnp.float32)
    place = lax.broadcasted_iota(jnp.int32, shape, 0)
    value, high = jnp.broadcast_to(value, shape), jnp.broadcast_to(high, shape)
    return jnp.where(place == 0, high, jnp.where(place == 1, value - high, 0.0)).astype(jnp.bfloat16)


def unpacked_loss(rows):
    rows = rows.astype(jnp.float32)
    return rows[0:1] + rows[1:2]


def early_kernel(which, later, kept, k1, g, g1, part):
    for slot, r in enumerate(which):
        column = 1 - later[r]
        for d in range(0, k1.shape[0], TILE):
            part[slot, d : d + TILE] = dot(kept[column, d : d + TILE], g[r], NN) + dot(k1[d : d + TILE], g1[r], NN)


def away_kernel(tb, i0, i1, i2, i3, text, part, l0, l1, grad, loss, out):
    scores(tb, (i0, i1, i2, i3), text[...].T, grad, loss)
    width = text.shape[0]
    for slot, r in enumerate((1, 3)):
        for d in range(0, width, TILE):
            out[slot, d : d + TILE] = (tb[0] * (part[slot, d : d + TILE] + dot(text[d : d + TILE], grad[r], NN))).astype(jnp.bfloat16)
        out[slot, width:] = packed_loss(l0[r : r + 1] + l1[r : r + 1] + loss[r : r + 1], (EXTRA, out.shape[2]))


def joined_kernel(tb, text, part, grad, l0, l1, l2, came, out):
    width = text.shape[0]
    for d in range(0, width, TILE):
        total = tb[0] * (part[2, d : d + TILE] + dot(text[d : d + TILE], grad[2], NN))
        out[d : d + TILE] = (total + came[1, d : d + TILE].astype(jnp.float32)).astype(jnp.bfloat16)
    loss = l0[2:3] + l1[2:3] + l2[2:3] + unpacked_loss(came[1, width:])
    out[width:] = packed_loss(loss, (EXTRA, out.shape[1]))


def home_kernel(tb, later, kept, x1, x2, g, g1, g2, l0, l1, l2, came, out, loss):
    width = x2.shape[0]
    for d in range(0, width, TILE):
        total = dot(kept[1 - later[0], d : d + TILE], g[0], NN) + dot(x1[d : d + TILE], g1[0], NN)
        total = tb[0] * (total + dot(x2[d : d + TILE], g2[0], NN))
        out[d : d + TILE] = total + came[0, d : d + TILE].astype(jnp.float32)
    loss[0:1] = l0[0:1] + l1[0:1] + l2[0:1] + unpacked_loss(came[0, width:])


def older_kernel(later, grad_m, returned, out):
    high = later[len(MASKS)] == 1
    out[...] = (grad_m[...] + jnp.where(high, returned[...].astype(jnp.float32), 0.0)).astype(jnp.bfloat16)


def last_kernel(parts, later, grad_t, r1, r2, p1, p2, home, loss, other, grad_image, losses, grad_text, image_buf, loss_buf, text_buf, sems):
    width, rows = grad_text.shape
    half, step = rows // 2, width // parts
    low = later[len(MASKS)] == 0
    f32 = jnp.float32
    copies = []

    def send(source, target):
        copy = pltpu.make_async_copy(source, target, sems.at[len(copies)])
        copy.start()
        copies.append(copy)

    for k in range(parts):
        d = pl.ds(k * step, step)
        image_buf[d] = home[d] + other[d].astype(f32)
        send(image_buf.at[d], grad_image.at[d])
    loss_buf[...] = (loss[0:1] + unpacked_loss(other[width:])) / float(rows)
    send(loss_buf, losses)
    for k in range(parts):
        d = pl.ds(k * step, step)
        text_buf[d, :half] = grad_t[d, :half] + jnp.where(low, r1[d].astype(f32), 0.0) + p1[d].astype(f32)
        text_buf[d, half:] = grad_t[d, half:] + jnp.where(low, r2[d].astype(f32), 0.0) + p2[d].astype(f32)
        send(text_buf.at[d], grad_text.at[d])
    for copy in copies:
        copy.wait()


def call(kernel, out_shape, args, scratch=(), flops=0, out_space=pltpu.VMEM):
    spaces = [pltpu.SMEM if a.ndim == 1 else pltpu.VMEM for a in args]
    return pl.pallas_call(
        kernel,
        out_shape=out_shape,
        in_specs=[pl.BlockSpec(memory_space=s) for s in spaces],
        out_specs=jax.tree.map(lambda _: pl.BlockSpec(memory_space=out_space), out_shape),
        scratch_shapes=list(scratch),
        cost_estimate=pl.CostEstimate(flops=flops, bytes_accessed=0, transcendentals=0) if flops else None,
        compiler_params=pltpu.CompilerParams(vmem_limit_bytes=VMEM_BYTES),
    )(*args)


def shards(image, text, scale, bias):
    width, rows = image.shape
    half = rows // 2
    f32, bf16 = jnp.float32, jnp.bfloat16
    sds = jax.ShapeDtypeStruct
    place = lax.axis_index(AXES) % WINDOW
    tb = jnp.concatenate([scale, bias])
    later = jnp.stack([((place ^ m) >= place).astype(jnp.int32) for m in MASKS] + [(place >= SIDE).astype(jnp.int32)])
    unit = 2 * rows * rows * width

    high = place >= SIDE
    cut = width // 256 * 128
    upper, lower = sds((cut, half), bf16), sds((width - cut, half), bf16)
    t1a, t1b, t2 = call(halves_kernel, (upper, lower, sds((width, half), bf16)), (text,))
    sent, t1a, t1b, t2 = lax.optimization_barrier((image, t1a, t1b, t2))
    m1a = moved(t1a, forward)
    m1b = moved(t1b, forward)
    m2 = moved(t2, forward)
    image_p = moved(sent, swap(PAIR))
    image_c = moved(sent, swap(CORE))
    x1a = moved(jnp.where(high, m1a, t1a), swap(SIDE))
    x1b = moved(jnp.where(high, m1b, t1b), swap(SIDE))
    x2 = moved(jnp.where(high, m2, t2), swap(SIDE))
    image_pc = moved(image_p, swap(CORE))
    images = (image, image_c, image_p, image_pc)

    grad_m1, grad_m2, g0, l0, kept = call(
        own_kernel,
        (
            sds((width, half), f32),
            sds((width, half), f32),
            sds((4, rows, rows), bf16),
            sds((8, rows), f32),
            sds((2, width, rows), bf16),
        ),
        (tb, later, *images, text, m1a, m1b, m2),
        scratch=(pltpu.VMEM((2, rows, width), bf16), pltpu.VMEM((4, rows, rows), bf16)),
    )
    x1a, x1b, _ = lax.optimization_barrier((x1a, x1b, l0))
    scored = (sds((4, half, rows), bf16), sds((8, rows), f32))
    grad_x1, g1, l1, x1 = call(partner_kernel, (sds((width, half), bf16), *scored, sds((width, half), bf16)), (tb, *images, x1a, x1b))
    part = call(functools.partial(early_kernel, (1, 3, 2)), sds((3, width, rows), f32), (later, kept, x1, g0, g1))
    g2, l2, away = call(away_kernel, (*scored, sds((2, width + EXTRA, rows), bf16)), (tb, *images, x2, part, l0, l1))
    came = moved(away, swap(CORE))
    grad_x2 = call(text_kernel, sds((width, half), bf16), (tb, *images, g2))
    r1 = moved(grad_x1, swap(SIDE))
    r2 = moved(grad_x2, swap(SIDE))

    older = sds((width, half), bf16)
    older1 = call(older_kernel, older, (later, grad_m1, r1), flops=80 * unit)
    _, held = lax.optimization_barrier((older1, l2))
    joined = call(joined_kernel, sds((width + EXTRA, rows), bf16), (tb, x2, part, g2, l0, l1, held, came), flops=0 * unit)
    other = moved(joined, swap(PAIR))
    older1, grad_m2, _ = lax.optimization_barrier((older1, grad_m2, joined))
    past1 = moved(older1, back)
    older2 = call(older_kernel, older, (later, grad_m2, r2), flops=20 * unit)
    past2 = moved(older2, back)
    _, late0 = lax.optimization_barrier((older2, g0))
    grad_t = call(
        own_text_kernel,
        sds((width, rows), f32),
        (tb, later, *images, late0),
        scratch=(pltpu.VMEM((4, rows, rows), bf16),),
    )
    _, late = lax.optimization_barrier((past1, l2))
    rest = (tb, later, kept, x1, x2, g0, g1, g2, l0, l1, late, came)
    home, home_loss = call(home_kernel, (sds((width, rows), f32), sds((8, rows), f32)), rest, flops=5 * unit)
    parts = 4
    grad_image, losses, grad_text = call(
        functools.partial(last_kernel, parts),
        (sds((width, rows), f32), sds((1, rows), f32), sds((width, rows), f32)),
        (later, grad_t, r1, r2, past1, past2, home, home_loss, other),
        scratch=(
            pltpu.VMEM((width, rows), f32),
            pltpu.VMEM((1, rows), f32),
            pltpu.VMEM((width, rows), f32),
            pltpu.SemaphoreType.DMA((2 * parts + 1,)),
        ),
        out_space=pl.ANY,
    )
    return grad_image, losses.reshape(rows), grad_text


def solution(mesh):
    spread = P(None, AXES)
    return jax.shard_map(
        shards,
        mesh=mesh,
        in_specs=(spread, spread, P(), P()),
        out_specs=(spread, P(AXES), spread),
        check_vma=False,
    )
```

```python
import functools

import jax
import jax.numpy as jnp
from jax import lax
from jax.experimental import pallas as pl
from jax.experimental.pallas import tpu as pltpu
from jax.sharding import PartitionSpec as P

AXES = ("dp", "mp")
WINDOW = 8
PAIR, CORE, SIDE = 1, 2, 4
MASKS = (0, CORE, PAIR, CORE | PAIR)
EXTRA = 16
TILE = 384
VMEM_BYTES = 20 * 1024 * 1024

NN = (((1,), (0,)), ((), ()))
NT = (((1,), (1,)), ((), ()))


def dot(a, b, dims):
    return lax.dot_general(a, b, dims, preferred_element_type=jnp.float32)


def moved(block, target):
    n = lax.axis_size(AXES)
    return lax.ppermute(block, AXES, [(i, target(i, n)) for i in range(n)])


def forward(i, n):
    return (i + WINDOW) % n


def back(i, n):
    return (i - WINDOW) % n


def swap(mask):
    return lambda i, n: i ^ mask


GROUP = 8


def terms(inner, tb):
    z = tb[0] * inner + tb[1]
    e = jnp.exp(-jnp.abs(z))
    u = 1.0 + e
    r = pl.reciprocal(u, approx=True)
    r = r * (2.0 - u * r)
    product = e[:GROUP]
    positive = jnp.maximum(z[:GROUP], 0.0)
    for d in range(GROUP, z.shape[0], GROUP):
        product = product * u[d : d + GROUP] + e[d : d + GROUP]
        positive = positive + jnp.maximum(z[d : d + GROUP], 0.0)
    soft = jnp.sum(jnp.log1p(product) + positive, axis=0, keepdims=True)
    return z, jnp.where(z >= 0, r, e * r), soft


def scores(tb, images, turned, grad, loss):
    for r, image in enumerate(images):
        _, s, soft = terms(dot(turned, image[...], NN), tb)
        grad[r] = s.astype(jnp.bfloat16)
        loss[r : r + 1] = soft


def text_side(tb, images, grad, out):
    for d in range(0, out.shape[0], TILE):
        total = dot(images[0][d : d + TILE], grad[0], NT)
        for r in (1, 2, 3):
            total = total + dot(images[r][d : d + TILE], grad[r], NT)
        out[d : d + TILE] = (tb[0] * total).astype(jnp.bfloat16)


def partner_kernel(tb, i0, i1, i2, i3, upper, lower, grad_x, grad, loss, text):
    cut = upper.shape[0]
    text[:cut] = upper[...]
    text[cut:] = lower[...]
    scores(tb, (i0, i1, i2, i3), text[...].T, grad, loss)
    text_side(tb, (i0, i1, i2, i3), grad, grad_x)


def text_kernel(tb, i0, i1, i2, i3, grad, grad_x):
    text_side(tb, (i0, i1, i2, i3), grad, grad_x)


def own_kernel(tb, later, i0, i1, i2, i3, text, m1a, m1b, m2, grad_m1, grad_m2, grad, loss, kept, turned, masked):
    temper = tb[0]
    rows = text.shape[1]
    half = rows // 2
    kept[0] = text[...]
    cut = m1a.shape[0]
    kept[1, :cut, :half] = m1a[...]
    kept[1, cut:, :half] = m1b[...]
    kept[1, :, half:] = m2[...]
    turned[0] = text[...].T
    turned[1, :half, :cut] = m1a[...].T
    turned[1, :half, cut:] = m1b[...].T
    turned[1, half:] = m2[...].T
    images = (i0, i1, i2, i3)
    for r, image in enumerate(images):
        same = later[r]
        z, s, soft = terms(dot(turned[1 - same], image[...], NN), tb)
        if r == 0:
            diag = lax.broadcasted_iota(jnp.int32, z.shape, 0) == lax.broadcasted_iota(jnp.int32, z.shape, 1)
            s = jnp.where(diag, s - 1.0, s)
            soft = soft - jnp.sum(jnp.where(diag, z, 0.0), axis=0, keepdims=True)
        g = s.astype(jnp.bfloat16)
        grad[r] = g
        loss[r : r + 1] = soft
        masked[r] = jnp.where(same == 1, jnp.zeros_like(g), g)
    for d in range(0, text.shape[0], TILE):
        total = dot(i1[d : d + TILE], masked[1], NT)
        for r in (2, 3):
            total = total + dot(images[r][d : d + TILE], masked[r], NT)
        total = temper * total
        grad_m1[d : d + TILE] = total[:, :half]
        grad_m2[d : d + TILE] = total[:, half:]


def own_text_kernel(tb, later, i0, i1, i2, i3, grad, r1, r2, first, second, masked):
    images = (i0, i1, i2, i3)
    half = r1.shape[1]
    low = later[len(MASKS)] == 0
    for r in (1, 2, 3):
        masked[r] = jnp.where(later[r] == 1, grad[r], jnp.zeros(grad.shape[1:], grad.dtype))
    for d in range(0, r1.shape[0], TILE):
        total = dot(i0[d : d + TILE], grad[0], NT)
        for r in (1, 2, 3):
            total = total + dot(images[r][d : d + TILE], masked[r], NT)
        total = tb[0] * total
        first[d : d + TILE] = total[:, :half] + jnp.where(low, r1[d : d + TILE].astype(jnp.float32), 0.0)
        second[d : d + TILE] = total[:, half:] + jnp.where(low, r2[d : d + TILE].astype(jnp.float32), 0.0)


def halves_kernel(text, upper, lower, second):
    half, cut = second.shape[1], upper.shape[0]
    upper[...] = text[:cut, :half]
    lower[...] = text[cut:, :half]
    second[...] = text[:, half:]


def packed_loss(value, shape):
    high = value.astype(jnp.bfloat16).astype(jnp.float32)
    place = lax.broadcasted_iota(jnp.int32, shape, 0)
    value, high = jnp.broadcast_to(value, shape), jnp.broadcast_to(high, shape)
    return jnp.where(place == 0, high, jnp.where(place == 1, value - high, 0.0)).astype(jnp.bfloat16)


def unpacked_loss(rows):
    rows = rows.astype(jnp.float32)
    return rows[0:1] + rows[1:2]


def early_kernel(which, later, kept, k1, g, g1, part):
    for slot, r in enumerate(which):
        column = 1 - later[r]
        for d in range(0, k1.shape[0], TILE):
            part[slot, d : d + TILE] = dot(kept[column, d : d + TILE], g[r], NN) + dot(k1[d : d + TILE], g1[r], NN)


def away_kernel(tb, i0, i1, i2, i3, text, part, l0, l1, grad, loss, out):
    scores(tb, (i0, i1, i2, i3), text[...].T, grad, loss)
    width = text.shape[0]
    for slot, r in enumerate((1, 3)):
        for d in range(0, width, TILE):
            out[slot, d : d + TILE] = (tb[0] * (part[slot, d : d + TILE] + dot(text[d : d + TILE], grad[r], NN))).astype(jnp.bfloat16)
        out[slot, width:] = packed_loss(l0[r : r + 1] + l1[r : r + 1] + loss[r : r + 1], (EXTRA, out.shape[2]))


def joined_kernel(tb, text, part, grad, l0, l1, l2, came, out):
    width = text.shape[0]
    for d in range(0, width, TILE):
        total = tb[0] * (part[2, d : d + TILE] + dot(text[d : d + TILE], grad[2], NN))
        out[d : d + TILE] = (total + came[1, d : d + TILE].astype(jnp.float32)).astype(jnp.bfloat16)
    loss = l0[2:3] + l1[2:3] + l2[2:3] + unpacked_loss(came[1, width:])
    out[width:] = packed_loss(loss, (EXTRA, out.shape[1]))


def home_kernel(tb, later, kept, x1, x2, g, g1, g2, l0, l1, l2, came, first, past, out, loss, text):
    width = x2.shape[0]
    for d in range(0, width, TILE):
        total = dot(kept[1 - later[0], d : d + TILE], g[0], NN) + dot(x1[d : d + TILE], g1[0], NN)
        total = tb[0] * (total + dot(x2[d : d + TILE], g2[0], NN))
        out[d : d + TILE] = total + came[0, d : d + TILE].astype(jnp.float32)
    loss[0:1] = l0[0:1] + l1[0:1] + l2[0:1] + unpacked_loss(came[0, width:])
    text[...] = first[...] + past[...].astype(jnp.float32)


def older_kernel(later, grad_m, returned, out):
    high = later[len(MASKS)] == 1
    out[...] = (grad_m[...] + jnp.where(high, returned[...].astype(jnp.float32), 0.0)).astype(jnp.bfloat16)


def last_kernel(parts, first, second, past, home, loss, other, grad_image, losses, grad_text, image_buf, loss_buf, text_buf, sems):
    width, rows = grad_text.shape
    half, step = rows // 2, width // parts
    f32 = jnp.float32
    copies = []

    def send(source, target):
        copy = pltpu.make_async_copy(source, target, sems.at[len(copies)])
        copy.start()
        copies.append(copy)

    send(first, grad_text.at[:, pl.ds(0, half)])
    for k in range(parts):
        d = pl.ds(k * step, step)
        image_buf[d] = home[d] + other[d].astype(f32)
        send(image_buf.at[d], grad_image.at[d])
    loss_buf[...] = (loss[0:1] + unpacked_loss(other[width:])) / float(rows)
    send(loss_buf, losses)
    for k in range(parts):
        d = pl.ds(k * step, step)
        text_buf[d] = second[d] + past[d].astype(f32)
        send(text_buf.at[d], grad_text.at[d, pl.ds(half, half)])
    for copy in copies:
        copy.wait()


def call(kernel, out_shape, args, scratch=(), flops=0, out_space=pltpu.VMEM):
    spaces = [pltpu.SMEM if a.ndim == 1 else pltpu.VMEM for a in args]
    return pl.pallas_call(
        kernel,
        out_shape=out_shape,
        in_specs=[pl.BlockSpec(memory_space=s) for s in spaces],
        out_specs=jax.tree.map(lambda _: pl.BlockSpec(memory_space=out_space), out_shape),
        scratch_shapes=list(scratch),
        cost_estimate=pl.CostEstimate(flops=flops, bytes_accessed=0, transcendentals=0) if flops else None,
        compiler_params=pltpu.CompilerParams(vmem_limit_bytes=VMEM_BYTES),
    )(*args)


def shards(image, text, scale, bias):
    width, rows = image.shape
    half = rows // 2
    f32, bf16 = jnp.float32, jnp.bfloat16
    sds = jax.ShapeDtypeStruct
    place = lax.axis_index(AXES) % WINDOW
    tb = jnp.concatenate([scale, bias])
    later = jnp.stack([((place ^ m) >= place).astype(jnp.int32) for m in MASKS] + [(place >= SIDE).astype(jnp.int32)])
    unit = 2 * rows * rows * width

    high = place >= SIDE
    cut = width // 256 * 128
    upper, lower = sds((cut, half), bf16), sds((width - cut, half), bf16)
    t1a, t1b, t2 = call(halves_kernel, (upper, lower, sds((width, half), bf16)), (text,))
    sent, t1a, t1b, t2 = lax.optimization_barrier((image, t1a, t1b, t2))
    m1a = moved(t1a, forward)
    m1b = moved(t1b, forward)
    m2 = moved(t2, forward)
    image_p = moved(sent, swap(PAIR))
    image_c = moved(sent, swap(CORE))
    x1a = moved(jnp.where(high, m1a, t1a), swap(SIDE))
    x1b = moved(jnp.where(high, m1b, t1b), swap(SIDE))
    x2 = moved(jnp.where(high, m2, t2), swap(SIDE))
    image_pc = moved(image_p, swap(CORE))
    images = (image, image_c, image_p, image_pc)

    grad_m1, grad_m2, g0, l0, kept = call(
        own_kernel,
        (
            sds((width, half), f32),
            sds((width, half), f32),
            sds((4, rows, rows), bf16),
            sds((8, rows), f32),
            sds((2, width, rows), bf16),
        ),
        (tb, later, *images, text, m1a, m1b, m2),
        scratch=(pltpu.VMEM((2, rows, width), bf16), pltpu.VMEM((4, rows, rows), bf16)),
    )
    x1a, x1b, _ = lax.optimization_barrier((x1a, x1b, l0))
    scored = (sds((4, half, rows), bf16), sds((8, rows), f32))
    grad_x1, g1, l1, x1 = call(partner_kernel, (sds((width, half), bf16), *scored, sds((width, half), bf16)), (tb, *images, x1a, x1b))
    part = call(functools.partial(early_kernel, (1, 3, 2)), sds((3, width, rows), f32), (later, kept, x1, g0, g1))
    g2, l2, away = call(away_kernel, (*scored, sds((2, width + EXTRA, rows), bf16)), (tb, *images, x2, part, l0, l1))
    came = moved(away, swap(CORE))
    grad_x2 = call(text_kernel, sds((width, half), bf16), (tb, *images, g2))
    r1 = moved(grad_x1, swap(SIDE))
    r2 = moved(grad_x2, swap(SIDE))

    older = sds((width, half), bf16)
    older1 = call(older_kernel, older, (later, grad_m1, r1), flops=80 * unit)
    _, held = lax.optimization_barrier((older1, l2))
    joined = call(joined_kernel, sds((width + EXTRA, rows), bf16), (tb, x2, part, g2, l0, l1, held, came), flops=0 * unit)
    other = moved(joined, swap(PAIR))
    older1, grad_m2, _ = lax.optimization_barrier((older1, grad_m2, joined))
    past1 = moved(older1, back)
    older2 = call(older_kernel, older, (later, grad_m2, r2), flops=20 * unit)
    past2 = moved(older2, back)
    _, late0 = lax.optimization_barrier((older2, g0))
    first, second = call(
        own_text_kernel,
        (sds((width, half), f32),) * 2,
        (tb, later, *images, late0, r1, r2),
        scratch=(pltpu.VMEM((4, rows, rows), bf16),),
    )
    _, late = lax.optimization_barrier((past1, l2))
    rest = (tb, later, kept, x1, x2, g0, g1, g2, l0, l1, late, came, first, past1)
    home, home_loss, first = call(home_kernel, (sds((width, rows), f32), sds((8, rows), f32), sds((width, half), f32)), rest, flops=5 * unit)
    parts = 4
    grad_image, losses, grad_text = call(
        functools.partial(last_kernel, parts),
        (sds((width, rows), f32), sds((1, rows), f32), sds((width, rows), f32)),
        (first, second, past2, home, home_loss, other),
        scratch=(
            pltpu.VMEM((width, rows), f32),
            pltpu.VMEM((1, rows), f32),
            pltpu.VMEM((width, half), f32),
            pltpu.SemaphoreType.DMA((2 * parts + 2,)),
        ),
        out_space=pl.ANY,
    )
    return grad_image, losses.reshape(rows), grad_text


def solution(mesh):
    spread = P(None, AXES)
    return jax.shard_map(
        shards,
        mesh=mesh,
        in_specs=(spread, spread, P(), P()),
        out_specs=(spread, P(AXES), spread),
        check_vma=False,
    )
```

```python
import functools

import jax
import jax.numpy as jnp
from jax import lax
from jax.experimental import pallas as pl
from jax.experimental.pallas import tpu as pltpu
from jax.sharding import PartitionSpec as P

AXES = ("dp", "mp")
WINDOW = 8
PAIR, CORE, SIDE = 1, 2, 4
MASKS = (0, CORE, PAIR, CORE | PAIR)
EXTRA = 16
TILE = 384
VMEM_BYTES = 20 * 1024 * 1024

NN = (((1,), (0,)), ((), ()))
NT = (((1,), (1,)), ((), ()))


def dot(a, b, dims):
    return lax.dot_general(a, b, dims, preferred_element_type=jnp.float32)


def moved(block, target):
    n = lax.axis_size(AXES)
    return lax.ppermute(block, AXES, [(i, target(i, n)) for i in range(n)])


def forward(i, n):
    return (i + WINDOW) % n


def back(i, n):
    return (i - WINDOW) % n


def swap(mask):
    return lambda i, n: i ^ mask


GROUP = 8


def terms(inner, tb):
    z = tb[0] * inner + tb[1]
    e = jnp.exp(-jnp.abs(z))
    u = 1.0 + e
    r = pl.reciprocal(u, approx=True)
    r = r * (2.0 - u * r)
    product = e[:GROUP]
    positive = jnp.maximum(z[:GROUP], 0.0)
    for d in range(GROUP, z.shape[0], GROUP):
        product = product * u[d : d + GROUP] + e[d : d + GROUP]
        positive = positive + jnp.maximum(z[d : d + GROUP], 0.0)
    soft = jnp.sum(jnp.log1p(product) + positive, axis=0, keepdims=True)
    return z, jnp.where(z >= 0, r, e * r), soft


def scores(tb, images, turned, grad, loss):
    for r, image in enumerate(images):
        _, s, soft = terms(dot(turned, image[...], NN), tb)
        grad[r] = s.astype(jnp.bfloat16)
        loss[r : r + 1] = soft


def text_side(tb, images, grad, out):
    for d in range(0, out.shape[0], TILE):
        total = dot(images[0][d : d + TILE], grad[0], NT)
        for r in (1, 2, 3):
            total = total + dot(images[r][d : d + TILE], grad[r], NT)
        out[d : d + TILE] = (tb[0] * total).astype(jnp.bfloat16)


def partner_kernel(tb, i0, i1, i2, i3, upper, lower, grad_x, grad, loss, text):
    cut = upper.shape[0]
    text[:cut] = upper[...]
    text[cut:] = lower[...]
    scores(tb, (i0, i1, i2, i3), text[...].T, grad, loss)
    text_side(tb, (i0, i1, i2, i3), grad, grad_x)


def text_kernel(tb, i0, i1, i2, i3, grad, grad_x):
    text_side(tb, (i0, i1, i2, i3), grad, grad_x)


def own_kernel(tb, later, i0, i1, i2, i3, text, m1a, m1b, m2, grad_m1, grad_m2, grad, loss, kept, turned, masked):
    temper = tb[0]
    rows = text.shape[1]
    half = rows // 2
    kept[0] = text[...]
    cut = m1a.shape[0]
    kept[1, :cut, :half] = m1a[...]
    kept[1, cut:, :half] = m1b[...]
    kept[1, :, half:] = m2[...]
    turned[0] = text[...].T
    turned[1, :half, :cut] = m1a[...].T
    turned[1, :half, cut:] = m1b[...].T
    turned[1, half:] = m2[...].T
    images = (i0, i1, i2, i3)
    for r, image in enumerate(images):
        same = later[r]
        z, s, soft = terms(dot(turned[1 - same], image[...], NN), tb)
        if r == 0:
            diag = lax.broadcasted_iota(jnp.int32, z.shape, 0) == lax.broadcasted_iota(jnp.int32, z.shape, 1)
            s = jnp.where(diag, s - 1.0, s)
            soft = soft - jnp.sum(jnp.where(diag, z, 0.0), axis=0, keepdims=True)
        g = s.astype(jnp.bfloat16)
        grad[r] = g
        loss[r : r + 1] = soft
        masked[r] = jnp.where(same == 1, jnp.zeros_like(g), g)
    for d in range(0, text.shape[0], TILE):
        total = dot(i1[d : d + TILE], masked[1], NT)
        for r in (2, 3):
            total = total + dot(images[r][d : d + TILE], masked[r], NT)
        total = temper * total
        grad_m1[d : d + TILE] = total[:, :half]
        grad_m2[d : d + TILE] = total[:, half:]


def own_text_kernel(tb, later, i0, i1, i2, i3, grad, r1, r2, first, second, masked):
    images = (i0, i1, i2, i3)
    half = r1.shape[1]
    low = later[len(MASKS)] == 0
    for r in (1, 2, 3):
        masked[r] = jnp.where(later[r] == 1, grad[r], jnp.zeros(grad.shape[1:], grad.dtype))
    for d in range(0, r1.shape[0], TILE):
        total = dot(i0[d : d + TILE], grad[0], NT)
        for r in (1, 2, 3):
            total = total + dot(images[r][d : d + TILE], masked[r], NT)
        total = tb[0] * total
        first[d : d + TILE] = total[:, :half] + jnp.where(low, r1[d : d + TILE].astype(jnp.float32), 0.0)
        second[d : d + TILE] = total[:, half:] + jnp.where(low, r2[d : d + TILE].astype(jnp.float32), 0.0)


def halves_kernel(text, upper, lower, second):
    half, cut = second.shape[1], upper.shape[0]
    upper[...] = text[:cut, :half]
    lower[...] = text[cut:, :half]
    second[...] = text[:, half:]


def packed_loss(value, shape):
    high = value.astype(jnp.bfloat16).astype(jnp.float32)
    place = lax.broadcasted_iota(jnp.int32, shape, 0)
    value, high = jnp.broadcast_to(value, shape), jnp.broadcast_to(high, shape)
    return jnp.where(place == 0, high, jnp.where(place == 1, value - high, 0.0)).astype(jnp.bfloat16)


def unpacked_loss(rows):
    rows = rows.astype(jnp.float32)
    return rows[0:1] + rows[1:2]


def early_kernel(which, later, kept, k1, g, g1, part):
    for slot, r in enumerate(which):
        column = 1 - later[r]
        for d in range(0, k1.shape[0], TILE):
            part[slot, d : d + TILE] = dot(kept[column, d : d + TILE], g[r], NN) + dot(k1[d : d + TILE], g1[r], NN)


def away_kernel(tb, i0, i1, i2, i3, text, part, l0, l1, grad, loss, out):
    scores(tb, (i0, i1, i2, i3), text[...].T, grad, loss)
    width = text.shape[0]
    for slot, r in enumerate((1, 3)):
        for d in range(0, width, TILE):
            out[slot, d : d + TILE] = (tb[0] * (part[slot, d : d + TILE] + dot(text[d : d + TILE], grad[r], NN))).astype(jnp.bfloat16)
        out[slot, width:] = packed_loss(l0[r : r + 1] + l1[r : r + 1] + loss[r : r + 1], (EXTRA, out.shape[2]))


def pair_kernel(tb, text, part, grad, out):
    for d in range(0, text.shape[0], TILE):
        out[d : d + TILE] = tb[0] * (part[2, d : d + TILE] + dot(text[d : d + TILE], grad[2], NN))


def joined_kernel(pair, l0, l1, l2, came, out):
    width = pair.shape[0]
    out[:width] = (pair[...] + came[1, :width].astype(jnp.float32)).astype(jnp.bfloat16)
    loss = l0[2:3] + l1[2:3] + l2[2:3] + unpacked_loss(came[1, width:])
    out[width:] = packed_loss(loss, (EXTRA, out.shape[1]))


def home_kernel(tb, later, kept, x1, x2, g, g1, g2, l0, l1, l2, came, first, past, out, loss, text):
    width = x2.shape[0]
    for d in range(0, width, TILE):
        total = dot(kept[1 - later[0], d : d + TILE], g[0], NN) + dot(x1[d : d + TILE], g1[0], NN)
        total = tb[0] * (total + dot(x2[d : d + TILE], g2[0], NN))
        out[d : d + TILE] = total + came[0, d : d + TILE].astype(jnp.float32)
    loss[0:1] = l0[0:1] + l1[0:1] + l2[0:1] + unpacked_loss(came[0, width:])
    text[...] = first[...] + past[...].astype(jnp.float32)


def older_kernel(later, grad_m, returned, out):
    high = later[len(MASKS)] == 1
    out[...] = (grad_m[...] + jnp.where(high, returned[...].astype(jnp.float32), 0.0)).astype(jnp.bfloat16)


def last_kernel(parts, first, second, past, home, loss, other, grad_image, losses, grad_text, image_buf, loss_buf, text_buf, sems):
    width, rows = grad_text.shape
    half, step = rows // 2, width // parts
    f32 = jnp.float32
    copies = []

    def send(source, target):
        copy = pltpu.make_async_copy(source, target, sems.at[len(copies)])
        copy.start()
        copies.append(copy)

    send(first, grad_text.at[:, pl.ds(0, half)])
    for k in range(parts):
        d = pl.ds(k * step, step)
        image_buf[d] = home[d] + other[d].astype(f32)
        send(image_buf.at[d], grad_image.at[d])
    loss_buf[...] = (loss[0:1] + unpacked_loss(other[width:])) / float(rows)
    send(loss_buf, losses)
    for k in range(parts):
        d = pl.ds(k * step, step)
        text_buf[d] = second[d] + past[d].astype(f32)
        send(text_buf.at[d], grad_text.at[d, pl.ds(half, half)])
    for copy in copies:
        copy.wait()


def call(kernel, out_shape, args, scratch=(), flops=0, out_space=pltpu.VMEM):
    spaces = [pltpu.SMEM if a.ndim == 1 else pltpu.VMEM for a in args]
    return pl.pallas_call(
        kernel,
        out_shape=out_shape,
        in_specs=[pl.BlockSpec(memory_space=s) for s in spaces],
        out_specs=jax.tree.map(lambda _: pl.BlockSpec(memory_space=out_space), out_shape),
        scratch_shapes=list(scratch),
        cost_estimate=pl.CostEstimate(flops=flops, bytes_accessed=0, transcendentals=0) if flops else None,
        compiler_params=pltpu.CompilerParams(vmem_limit_bytes=VMEM_BYTES),
    )(*args)


def shards(image, text, scale, bias):
    width, rows = image.shape
    half = rows // 2
    f32, bf16 = jnp.float32, jnp.bfloat16
    sds = jax.ShapeDtypeStruct
    place = lax.axis_index(AXES) % WINDOW
    tb = jnp.concatenate([scale, bias])
    later = jnp.stack([((place ^ m) >= place).astype(jnp.int32) for m in MASKS] + [(place >= SIDE).astype(jnp.int32)])
    unit = 2 * rows * rows * width

    high = place >= SIDE
    cut = width // 256 * 128
    upper, lower = sds((cut, half), bf16), sds((width - cut, half), bf16)
    t1a, t1b, t2 = call(halves_kernel, (upper, lower, sds((width, half), bf16)), (text,))
    sent, t1a, t1b, t2 = lax.optimization_barrier((image, t1a, t1b, t2))
    m1a = moved(t1a, forward)
    m1b = moved(t1b, forward)
    m2 = moved(t2, forward)
    image_p = moved(sent, swap(PAIR))
    image_c = moved(sent, swap(CORE))
    x1a = moved(jnp.where(high, m1a, t1a), swap(SIDE))
    x1b = moved(jnp.where(high, m1b, t1b), swap(SIDE))
    x2 = moved(jnp.where(high, m2, t2), swap(SIDE))
    image_pc = moved(image_p, swap(CORE))
    images = (image, image_c, image_p, image_pc)

    grad_m1, grad_m2, g0, l0, kept = call(
        own_kernel,
        (
            sds((width, half), f32),
            sds((width, half), f32),
            sds((4, rows, rows), bf16),
            sds((8, rows), f32),
            sds((2, width, rows), bf16),
        ),
        (tb, later, *images, text, m1a, m1b, m2),
        scratch=(pltpu.VMEM((2, rows, width), bf16), pltpu.VMEM((4, rows, rows), bf16)),
    )
    x1a, x1b, _ = lax.optimization_barrier((x1a, x1b, l0))
    scored = (sds((4, half, rows), bf16), sds((8, rows), f32))
    grad_x1, g1, l1, x1 = call(partner_kernel, (sds((width, half), bf16), *scored, sds((width, half), bf16)), (tb, *images, x1a, x1b))
    part = call(functools.partial(early_kernel, (1, 3, 2)), sds((3, width, rows), f32), (later, kept, x1, g0, g1))
    g2, l2, away = call(away_kernel, (*scored, sds((2, width + EXTRA, rows), bf16)), (tb, *images, x2, part, l0, l1))
    came = moved(away, swap(CORE))
    grad_x2 = call(text_kernel, sds((width, half), bf16), (tb, *images, g2))
    r1 = moved(grad_x1, swap(SIDE))
    r2 = moved(grad_x2, swap(SIDE))

    older = sds((width, half), bf16)
    _, after = lax.optimization_barrier((grad_x2, g2))
    pair = call(pair_kernel, sds((width, rows), f32), (tb, x2, part, after))
    grad_m1, pair = lax.optimization_barrier((grad_m1, pair))
    older1 = call(older_kernel, older, (later, grad_m1, r1), flops=80 * unit)
    _, held = lax.optimization_barrier((older1, l2))
    joined = call(joined_kernel, sds((width + EXTRA, rows), bf16), (pair, l0, l1, held, came), flops=0 * unit)
    other = moved(joined, swap(PAIR))
    older1, grad_m2, _ = lax.optimization_barrier((older1, grad_m2, joined))
    past1 = moved(older1, back)
    older2 = call(older_kernel, older, (later, grad_m2, r2), flops=20 * unit)
    past2 = moved(older2, back)
    _, late0 = lax.optimization_barrier((older2, g0))
    first, second = call(
        own_text_kernel,
        (sds((width, half), f32),) * 2,
        (tb, later, *images, late0, r1, r2),
        scratch=(pltpu.VMEM((4, rows, rows), bf16),),
    )
    _, late = lax.optimization_barrier((past1, l2))
    rest = (tb, later, kept, x1, x2, g0, g1, g2, l0, l1, late, came, first, past1)
    home, home_loss, first = call(home_kernel, (sds((width, rows), f32), sds((8, rows), f32), sds((width, half), f32)), rest, flops=5 * unit)
    parts = 4
    grad_image, losses, grad_text = call(
        functools.partial(last_kernel, parts),
        (sds((width, rows), f32), sds((1, rows), f32), sds((width, rows), f32)),
        (first, second, past2, home, home_loss, other),
        scratch=(
            pltpu.VMEM((width, rows), f32),
            pltpu.VMEM((1, rows), f32),
            pltpu.VMEM((width, half), f32),
            pltpu.SemaphoreType.DMA((2 * parts + 2,)),
        ),
        out_space=pl.ANY,
    )
    return grad_image, losses.reshape(rows), grad_text


def solution(mesh):
    spread = P(None, AXES)
    return jax.shard_map(
        shards,
        mesh=mesh,
        in_specs=(spread, spread, P(), P()),
        out_specs=(spread, P(AXES), spread),
        check_vma=False,
    )
```

```python
import functools

import jax
import jax.numpy as jnp
from jax import lax
from jax.experimental import pallas as pl
from jax.experimental.pallas import tpu as pltpu
from jax.sharding import PartitionSpec as P

AXES = ("dp", "mp")
WINDOW = 8
PAIR, CORE, SIDE = 1, 2, 4
MASKS = (0, CORE, PAIR, CORE | PAIR)
EXTRA = 16
TILE = 384
VMEM_BYTES = 20 * 1024 * 1024

NN = (((1,), (0,)), ((), ()))
NT = (((1,), (1,)), ((), ()))


def dot(a, b, dims):
    return lax.dot_general(a, b, dims, preferred_element_type=jnp.float32)


def moved(block, target):
    n = lax.axis_size(AXES)
    return lax.ppermute(block, AXES, [(i, target(i, n)) for i in range(n)])


def forward(i, n):
    return (i + WINDOW) % n


def back(i, n):
    return (i - WINDOW) % n


def swap(mask):
    return lambda i, n: i ^ mask


GROUP = 8


def terms(inner, tb):
    z = tb[0] * inner + tb[1]
    e = jnp.exp(-jnp.abs(z))
    u = 1.0 + e
    r = pl.reciprocal(u, approx=True)
    r = r * (2.0 - u * r)
    product = e[:GROUP]
    positive = jnp.maximum(z[:GROUP], 0.0)
    for d in range(GROUP, z.shape[0], GROUP):
        product = product * u[d : d + GROUP] + e[d : d + GROUP]
        positive = positive + jnp.maximum(z[d : d + GROUP], 0.0)
    soft = jnp.sum(jnp.log1p(product) + positive, axis=0, keepdims=True)
    return z, jnp.where(z >= 0, r, e * r), soft


def scores(tb, images, turned, grad, loss):
    for r, image in enumerate(images):
        _, s, soft = terms(dot(turned, image[...], NN), tb)
        grad[r] = s.astype(jnp.bfloat16)
        loss[r : r + 1] = soft


def text_side(tb, images, grad, out):
    for d in range(0, out.shape[0], TILE):
        total = dot(images[0][d : d + TILE], grad[0], NT)
        for r in (1, 2, 3):
            total = total + dot(images[r][d : d + TILE], grad[r], NT)
        out[d : d + TILE] = (tb[0] * total).astype(jnp.bfloat16)


def partner_kernel(tb, i0, i1, i2, i3, upper, lower, grad_x, grad, loss, text):
    cut = upper.shape[0]
    text[:cut] = upper[...]
    text[cut:] = lower[...]
    scores(tb, (i0, i1, i2, i3), text[...].T, grad, loss)
    text_side(tb, (i0, i1, i2, i3), grad, grad_x)


def text_kernel(tb, i0, i1, i2, i3, grad, grad_x):
    text_side(tb, (i0, i1, i2, i3), grad, grad_x)


def own_kernel(tb, later, i0, i1, i2, i3, text, m1a, m1b, m2, grad_m1, grad_m2, grad, loss, kept, turned, masked):
    temper = tb[0]
    rows = text.shape[1]
    half = rows // 2
    kept[0] = text[...]
    cut = m1a.shape[0]
    kept[1, :cut, :half] = m1a[...]
    kept[1, cut:, :half] = m1b[...]
    kept[1, :, half:] = m2[...]
    turned[0] = text[...].T
    turned[1, :half, :cut] = m1a[...].T
    turned[1, :half, cut:] = m1b[...].T
    turned[1, half:] = m2[...].T
    images = (i0, i1, i2, i3)
    for r, image in enumerate(images):
        same = later[r]
        z, s, soft = terms(dot(turned[1 - same], image[...], NN), tb)
        if r == 0:
            diag = lax.broadcasted_iota(jnp.int32, z.shape, 0) == lax.broadcasted_iota(jnp.int32, z.shape, 1)
            s = jnp.where(diag, s - 1.0, s)
            soft = soft - jnp.sum(jnp.where(diag, z, 0.0), axis=0, keepdims=True)
        g = s.astype(jnp.bfloat16)
        grad[r] = g
        loss[r : r + 1] = soft
        masked[r] = jnp.where(same == 1, jnp.zeros_like(g), g)
    for d in range(0, text.shape[0], TILE):
        total = dot(i1[d : d + TILE], masked[1], NT)
        for r in (2, 3):
            total = total + dot(images[r][d : d + TILE], masked[r], NT)
        total = temper * total
        grad_m1[d : d + TILE] = total[:, :half]
        grad_m2[d : d + TILE] = total[:, half:]


def own_text_kernel(tb, later, i0, i1, i2, i3, grad, r1, r2, first, second, masked):
    images = (i0, i1, i2, i3)
    half = r1.shape[1]
    low = later[len(MASKS)] == 0
    for r in (1, 2, 3):
        masked[r] = jnp.where(later[r] == 1, grad[r], jnp.zeros(grad.shape[1:], grad.dtype))
    for d in range(0, r1.shape[0], TILE):
        total = dot(i0[d : d + TILE], grad[0], NT)
        for r in (1, 2, 3):
            total = total + dot(images[r][d : d + TILE], masked[r], NT)
        total = tb[0] * total
        first[d : d + TILE] = total[:, :half] + jnp.where(low, r1[d : d + TILE].astype(jnp.float32), 0.0)
        second[d : d + TILE] = total[:, half:] + jnp.where(low, r2[d : d + TILE].astype(jnp.float32), 0.0)


def halves_kernel(text, upper, lower, second):
    half, cut = second.shape[1], upper.shape[0]
    upper[...] = text[:cut, :half]
    lower[...] = text[cut:, :half]
    second[...] = text[:, half:]


def packed_loss(value, shape):
    high = value.astype(jnp.bfloat16).astype(jnp.float32)
    place = lax.broadcasted_iota(jnp.int32, shape, 0)
    value, high = jnp.broadcast_to(value, shape), jnp.broadcast_to(high, shape)
    return jnp.where(place == 0, high, jnp.where(place == 1, value - high, 0.0)).astype(jnp.bfloat16)


def unpacked_loss(rows):
    rows = rows.astype(jnp.float32)
    return rows[0:1] + rows[1:2]


def early_kernel(which, later, kept, k1, g, g1, part):
    for slot, r in enumerate(which):
        column = 1 - later[r]
        for d in range(0, k1.shape[0], TILE):
            part[slot, d : d + TILE] = dot(kept[column, d : d + TILE], g[r], NN) + dot(k1[d : d + TILE], g1[r], NN)


def away_kernel(tb, i0, i1, i2, i3, text, part, l0, l1, grad, loss, out):
    scores(tb, (i0, i1, i2, i3), text[...].T, grad, loss)
    width = text.shape[0]
    for slot, r in enumerate((1, 3)):
        for d in range(0, width, TILE):
            out[slot, d : d + TILE] = (tb[0] * (part[slot, d : d + TILE] + dot(text[d : d + TILE], grad[r], NN))).astype(jnp.bfloat16)
        out[slot, width:] = packed_loss(l0[r : r + 1] + l1[r : r + 1] + loss[r : r + 1], (EXTRA, out.shape[2]))


def pair_kernel(tb, text, part, grad, out):
    for d in range(0, text.shape[0], TILE):
        out[d : d + TILE] = tb[0] * (part[2, d : d + TILE] + dot(text[d : d + TILE], grad[2], NN))


def joined_kernel(pair, l0, l1, l2, came, out):
    width = pair.shape[0]
    out[:width] = (pair[...] + came[1, :width].astype(jnp.float32)).astype(jnp.bfloat16)
    loss = l0[2:3] + l1[2:3] + l2[2:3] + unpacked_loss(came[1, width:])
    out[width:] = packed_loss(loss, (EXTRA, out.shape[1]))


def home_kernel(tb, later, kept, x1, x2, g, g1, g2, l0, l1, l2, came, first, past, out, loss, text):
    width = x2.shape[0]
    for d in range(0, width, TILE):
        total = dot(kept[1 - later[0], d : d + TILE], g[0], NN) + dot(x1[d : d + TILE], g1[0], NN)
        total = tb[0] * (total + dot(x2[d : d + TILE], g2[0], NN))
        out[d : d + TILE] = total + came[0, d : d + TILE].astype(jnp.float32)
    loss[0:1] = l0[0:1] + l1[0:1] + l2[0:1] + unpacked_loss(came[0, width:])
    text[...] = first[...] + past[...].astype(jnp.float32)


def older_kernel(later, grad_m, returned, out):
    high = later[len(MASKS)] == 1
    out[...] = (grad_m[...] + jnp.where(high, returned[...].astype(jnp.float32), 0.0)).astype(jnp.bfloat16)


def last_kernel(parts, first, second, past, home, loss, other, grad_image, losses, grad_text, image_buf, loss_buf, text_buf, sems):
    width, rows = grad_text.shape
    half, step = rows // 2, width // parts
    f32 = jnp.float32
    copies = []

    def send(source, target):
        copy = pltpu.make_async_copy(source, target, sems.at[len(copies)])
        copy.start()
        copies.append(copy)

    send(first, grad_text.at[:, pl.ds(0, half)])
    for k in range(parts):
        d = pl.ds(k * step, step)
        image_buf[d] = home[d] + other[d].astype(f32)
        send(image_buf.at[d], grad_image.at[d])
    loss_buf[...] = (loss[0:1] + unpacked_loss(other[width:])) / float(rows)
    send(loss_buf, losses)
    for k in range(parts):
        d = pl.ds(k * step, step)
        text_buf[d] = second[d] + past[d].astype(f32)
        send(text_buf.at[d], grad_text.at[d, pl.ds(half, half)])
    for copy in copies:
        copy.wait()


def call(kernel, out_shape, args, scratch=(), flops=0, out_space=pltpu.VMEM):
    spaces = [pltpu.SMEM if a.ndim == 1 else pltpu.VMEM for a in args]
    return pl.pallas_call(
        kernel,
        out_shape=out_shape,
        in_specs=[pl.BlockSpec(memory_space=s) for s in spaces],
        out_specs=jax.tree.map(lambda _: pl.BlockSpec(memory_space=out_space), out_shape),
        scratch_shapes=list(scratch),
        cost_estimate=pl.CostEstimate(flops=flops, bytes_accessed=0, transcendentals=0) if flops else None,
        compiler_params=pltpu.CompilerParams(vmem_limit_bytes=VMEM_BYTES),
    )(*args)


def shards(image, text, scale, bias):
    width, rows = image.shape
    half = rows // 2
    f32, bf16 = jnp.float32, jnp.bfloat16
    sds = jax.ShapeDtypeStruct
    place = lax.axis_index(AXES) % WINDOW
    tb = jnp.concatenate([scale, bias])
    later = jnp.stack([((place ^ m) >= place).astype(jnp.int32) for m in MASKS] + [(place >= SIDE).astype(jnp.int32)])
    unit = 2 * rows * rows * width

    high = place >= SIDE
    cut = width // 256 * 128
    upper, lower = sds((cut, half), bf16), sds((width - cut, half), bf16)
    t1a, t1b, t2 = call(halves_kernel, (upper, lower, sds((width, half), bf16)), (text,))
    sent, t1a, t1b, t2 = lax.optimization_barrier((image, t1a, t1b, t2))
    m1a = moved(t1a, forward)
    m1b = moved(t1b, forward)
    m2 = moved(t2, forward)
    image_p = moved(sent, swap(PAIR))
    image_c = moved(sent, swap(CORE))
    x1a = moved(jnp.where(high, m1a, t1a), swap(SIDE))
    x1b = moved(jnp.where(high, m1b, t1b), swap(SIDE))
    x2 = moved(jnp.where(high, m2, t2), swap(SIDE))
    image_pc = moved(image_p, swap(CORE))
    images = (image, image_c, image_p, image_pc)

    grad_m1, grad_m2, g0, l0, kept = call(
        own_kernel,
        (
            sds((width, half), f32),
            sds((width, half), f32),
            sds((4, rows, rows), bf16),
            sds((8, rows), f32),
            sds((2, width, rows), bf16),
        ),
        (tb, later, *images, text, m1a, m1b, m2),
        scratch=(pltpu.VMEM((2, rows, width), bf16), pltpu.VMEM((4, rows, rows), bf16)),
    )
    x1a, x1b, _ = lax.optimization_barrier((x1a, x1b, l0))
    scored = (sds((4, half, rows), bf16), sds((8, rows), f32))
    grad_x1, g1, l1, x1 = call(partner_kernel, (sds((width, half), bf16), *scored, sds((width, half), bf16)), (tb, *images, x1a, x1b))
    part = call(functools.partial(early_kernel, (1, 3, 2)), sds((3, width, rows), f32), (later, kept, x1, g0, g1))
    g2, l2, away = call(away_kernel, (*scored, sds((2, width + EXTRA, rows), bf16)), (tb, *images, x2, part, l0, l1))
    came = moved(away, swap(CORE))
    grad_x2 = call(text_kernel, sds((width, half), bf16), (tb, *images, g2))
    r1 = moved(grad_x1, swap(SIDE))
    r2 = moved(grad_x2, swap(SIDE))

    older = sds((width, half), bf16)
    _, after = lax.optimization_barrier((grad_x2, g2))
    pair = call(pair_kernel, sds((width, rows), f32), (tb, x2, part, after))
    grad_m1, pair = lax.optimization_barrier((grad_m1, pair))
    older1 = call(older_kernel, older, (later, grad_m1, r1), flops=80 * unit)
    _, held = lax.optimization_barrier((older1, l2))
    joined = call(joined_kernel, sds((width + EXTRA, rows), bf16), (pair, l0, l1, held, came), flops=0 * unit)
    other = moved(joined, swap(PAIR))
    older1, grad_m2, _ = lax.optimization_barrier((older1, grad_m2, joined))
    past1 = moved(older1, back)
    older2 = (grad_m2 + jnp.where(high, r2.astype(f32), 0.0)).astype(bf16)
    past2 = moved(older2, back)
    _, late0 = lax.optimization_barrier((older2, g0))
    first, second = call(
        own_text_kernel,
        (sds((width, half), f32),) * 2,
        (tb, later, *images, late0, r1, r2),
        scratch=(pltpu.VMEM((4, rows, rows), bf16),),
    )
    _, late = lax.optimization_barrier((past1, l2))
    rest = (tb, later, kept, x1, x2, g0, g1, g2, l0, l1, late, came, first, past1)
    home, home_loss, first = call(home_kernel, (sds((width, rows), f32), sds((8, rows), f32), sds((width, half), f32)), rest, flops=5 * unit)
    parts = 4
    grad_image, losses, grad_text = call(
        functools.partial(last_kernel, parts),
        (sds((width, rows), f32), sds((1, rows), f32), sds((width, rows), f32)),
        (first, second, past2, home, home_loss, other),
        scratch=(
            pltpu.VMEM((width, rows), f32),
            pltpu.VMEM((1, rows), f32),
            pltpu.VMEM((width, half), f32),
            pltpu.SemaphoreType.DMA((2 * parts + 2,)),
        ),
        out_space=pl.ANY,
    )
    return grad_image, losses.reshape(rows), grad_text


def solution(mesh):
    spread = P(None, AXES)
    return jax.shard_map(
        shards,
        mesh=mesh,
        in_specs=(spread, spread, P(), P()),
        out_specs=(spread, P(AXES), spread),
        check_vma=False,
    )
```
